32 devices in a mesh: blk: 8 (over z, x), blade: 4 (over y, core).
Axes of the slice: x: 2, y: 2, z: 4, core: 2. Of those that a mesh axis runs over, the one named last changes fastest.
Arguments:
- bnd_pos: float32 [3, 2048], P(None, 'blk'), may hold values from -1 to 1
- bnd_owner: int32 [2048, 1], P('blk'), may hold values from 0 to 7; in each aligned block of 256 rows (0 to 255, 256 to 511, ...) at most 64 rows name the same one
- bnd_slot: int32 [2048], P('blk'), may hold values from 0 to 16383
- seg_start: float32 [3, 4, 1024], P(None, 'blade', 'blk'), may hold values from -1 to 1
- seg_step: float32 [3, 4, 1024], P(None, 'blade', 'blk'), may hold values from -0.15 to 0.15
- seg_gamma: float32 [4, 1024], P('blade', 'blk'), may hold values from -6 to 6
- seg_sec: int32 [4, 1024], P('blade', 'blk'), may hold values from 0 to 63
- flow: float32 [3, 64, 64, 256], P(None, 'blk', 'blade'), may hold values from -6 to 6
- source: float32 [3, 64, 64, 256], P(None, 'blk', 'blade'), may hold values from -6 to 6
- extra_diag: float32 [64, 64, 256], P('blk', 'blade'), may hold values from 0.25 to 2
- circ_weight: float32 [64, 64, 256], P('blk', 'blade'), may hold values from -0.125 to 0.125
- sec_block: int32 [4, 64], replicated, may hold values from 0 to 7
- sec_row: int32 [4, 64], replicated, may hold values from 0 to 15
Outputs:
- new_flow: float32 [3, 64, 64, 256], P(None, 'blk', 'blade')
- new_gamma: float32 [4, 1024], P('blade', 'blk')
The draws below stay inside these ranges and needn't reach their ends.
Inputs may be any that keep to these rules, and one draw needn't show every extreme that they name: `bnd_owner`: among the 256 boundary cells of each aligned block (one index of blk), at most 64 have the same owner, and some owner has exactly 64.
All inputs are finite; a program needn't handle non-finite values.
Results may differ from the reference program's by a relative error of at most 0.0001.
Values sent between devices are 32-bit elements; how exact they have to be, the bound alone decides.
A program may use at most 64 MiB of HBM per device.

```python
import math
import jax
import jax.numpy as jnp
import numpy as np
from jax import lax

NB_DEV = 256
CX = 8
CY = 16
CZ = 256
NSEC = 64
PASSES = 2
BLADES = 4
NB = 2048
SEGB = 1024
NX = 64
NY = 64
CAP = 64
N_BLK = 8


def with_ends(values, key, smallest, top_value):
    longest = values.shape.index(max(values.shape))
    spots = []
    for shift in (0, 1):
        where = [jax.random.randint(jax.random.fold_in(key, axis), (), 0, length) for axis, length in enumerate(values.shape)]
        where[longest] = (where[longest] + shift) % values.shape[longest]
        spots.append(tuple(where))
    return values.at[spots[0]].set(smallest).at[spots[1]].set(top_value)


def steps_of(own_key, extent, pieces, least, top_value):
    level = 1.0
    for axis_at, shards_of in pieces:
        draws = jax.random.uniform(jax.random.fold_in(jax.random.fold_in(own_key, 6), axis_at), (shards_of,), jnp.float32, least / len(pieces), top_value / len(pieces))
        level = level * jnp.repeat(jnp.exp(draws), extent[axis_at] // shards_of).reshape((-1,) + (1,) * (len(extent) - 1 - axis_at))
    return level


def deal_out(own_key, own, number, rows, number_of, top, bound, skew):
    order = jax.random.permutation(own_key, number_of)
    heavy_load, common = portions_of(number_of, rows * top, bound, skew, True), portions_of(number_of, rows * top, bound, skew, False)
    places = jnp.arange(number_of)

    def named(sizes, rotation):
        used = int((sizes > 0).sum())
        fixed = max(1, used // 4)
        passed = fixed + (places - fixed + rotation * (used - fixed)) % max(1, number_of - fixed)
        return jnp.zeros((number_of,), jnp.int32).at[order[jnp.where(places < fixed, places, passed)]].set(jnp.asarray(sizes, jnp.int32))

    sizes = jnp.where(number % 4 == 0, named(heavy_load, number // 4), named(common, number - number // 4 - 1))
    mixed = jax.random.permutation(jax.random.fold_in(own, 3), number_of)
    source_of, taker = mixed[0:number_of // 2 * 2:2], mixed[1:number_of // 2 * 2:2]
    margin = jnp.minimum(sizes[source_of] - 1, bound - sizes[taker]) // 2
    margin = jnp.where((source_of == order[0]) | (taker == order[0]) | (sizes[taker] == 0), 0, jnp.maximum(margin, 0))
    passed = jax.random.randint(jax.random.fold_in(own, 4), (number_of // 2,), 0, 1 << 20) % (margin + 1)
    sizes = sizes.at[source_of].add(-passed).at[taker].add(passed)
    items = jnp.searchsorted(jnp.cumsum(sizes), jnp.arange(rows * top), side="right").astype(jnp.int32)
    table = items.reshape(top, rows).T
    table = table[jax.random.permutation(jax.random.fold_in(own, 1), rows)]
    rotation = jax.random.randint(jax.random.fold_in(own, 2), (rows, 1), 0, top)
    return jnp.take_along_axis(table, (jnp.arange(top)[None, :] + rotation) % top, axis=1)


def portions_of(count, total, reach, lean, full):
    loads = [(1 << 20) // math.isqrt(standing ** lean) + 1 for standing in range(1, count + 1)]
    largest = reach if full else min(reach, max(-(-total // count), total * loads[0] // sum(loads)))
    least = 1 if total - largest >= count - 1 else 0
    holding, spare = [largest] + [least] * (count - 1), total - largest - least * (count - 1)
    while spare > 0:
        free = [i for i in range(1, count) if holding[i] < largest] or [i for i in range(1, count) if holding[i] < reach]
        whole, left = sum([loads[i] for i in free]), spare
        for i in free:
            addition = min(reach - holding[i], max(1, left * loads[i] // whole), spare)
            holding[i] = holding[i] + addition
            spare = spare - addition
    return np.array(holding)


def centred(own_key, dims, scale, bound, pieces=(), kind=jnp.bfloat16):
    drawn = jax.random.normal(own_key, dims, jnp.float32) * scale
    if len(pieces) > 0:
        drawn = steps_of(own_key, dims, pieces, -0.22, 0.18) * drawn
    return jnp.clip(drawn, min=-bound, max=bound).astype(kind)


def setup_inputs(seed: int = 0) -> dict:
    streams_of = jax.random.split(jax.random.key(seed), 14)
    bnd_pos = jnp.clip(jax.random.uniform(streams_of[0], (3, NB), jnp.float32, -1.0, 1.0) * steps_of(streams_of[0], (3, NB), ((1, 8),), -0.4, 0.0), -1.0, 1.0)
    bnd_owner_keys = jax.random.split(jax.random.fold_in(streams_of[1], 1), NB // NB_DEV)
    bnd_owner_turns = jax.random.permutation(jax.random.fold_in(streams_of[1], 3), NB // NB_DEV)
    bnd_owner = jax.vmap(lambda own, number: deal_out(jax.random.fold_in(streams_of[1], 2), own, number, NB_DEV, N_BLK, 1, CAP, 2))(bnd_owner_keys, bnd_owner_turns).reshape((NB, 1))
    bnd_slot = with_ends(jax.random.randint(streams_of[2], (NB,), 0, NY * CZ), jax.random.fold_in(streams_of[2], 1), 0, (NY * CZ) - 1).astype(jnp.int32)
    seg_start = jnp.clip(jax.random.uniform(streams_of[3], (3, BLADES, SEGB), jnp.float32, -1.0, 1.0) * steps_of(streams_of[3], (3, BLADES, SEGB), ((1, 4), (2, 8)), -0.4, 0.0), -1.0, 1.0)
    seg_step = jnp.clip(jax.random.uniform(streams_of[4], (3, BLADES, SEGB), jnp.float32, -0.15, 0.15) * steps_of(streams_of[4], (3, BLADES, SEGB), ((1, 4), (2, 8)), -0.4, 0.0), -0.15, 0.15)
    seg_gamma = centred(streams_of[5], (BLADES, SEGB), 1.0, 6.0, ((0, 4), (1, 8)), jnp.float32)
    seg_sec = with_ends(jax.random.randint(streams_of[6], (BLADES, SEGB), 0, NSEC), jax.random.fold_in(streams_of[6], 1), 0, NSEC - 1).astype(jnp.int32)
    flow = centred(streams_of[7], (3, NX, NY, CZ), 1.0, 6.0, ((1, 8), (2, 4)), jnp.float32)
    source = centred(streams_of[8], (3, NX, NY, CZ), 1.0, 6.0, ((1, 8), (2, 4)), jnp.float32)
    extra_diag = jnp.clip(0.25 + 1.75 * jax.random.uniform(streams_of[9], (NX, NY, CZ), jnp.float32) ** steps_of(streams_of[9], (NX, NY, CZ), ((0, 8), (1, 4)), -0.2, 0.2), 0.25, 2.0)
    circ_weight = centred(streams_of[10], (NX, NY, CZ), (CX * CZ) ** -0.5, 0.125, ((0, 8), (1, 4)), jnp.float32)
    sec_block = with_ends(jax.random.randint(streams_of[11], (BLADES, NSEC), 0, N_BLK), jax.random.fold_in(streams_of[11], 1), 0, N_BLK - 1).astype(jnp.int32)
    sec_row = with_ends(jax.random.randint(streams_of[12], (BLADES, NSEC), 0, CY), jax.random.fold_in(streams_of[12], 1), 0, CY - 1).astype(jnp.int32)
    return dict(bnd_pos=bnd_pos, bnd_owner=bnd_owner, bnd_slot=bnd_slot, seg_start=seg_start, seg_step=seg_step, seg_gamma=seg_gamma, seg_sec=seg_sec, flow=flow, source=source, extra_diag=extra_diag, circ_weight=circ_weight, sec_block=sec_block, sec_row=sec_row)


CORE = 0.01
FOUR_PI = 4.0 * math.pi
OMEGA = 0.8
RELAX = 0.5

def pair_velocity(points, segs):
    p = points[:, :, None]
    start = segs[0:3, None, :]
    step = segs[3:6, None, :]
    gamma = segs[6][None, :]
    r1 = p - start
    r2 = r1 - step
    cross_x = r1[1] * r2[2] - r1[2] * r2[1]
    cross_y = r1[2] * r2[0] - r1[0] * r2[2]
    cross_z = r1[0] * r2[1] - r1[1] * r2[0]
    cross_sq = cross_x * cross_x + cross_y * cross_y + cross_z * cross_z
    norm_one = jnp.sqrt(lax.optimization_barrier(jnp.sum(r1 * r1, 0)) + CORE)
    norm_two = jnp.sqrt(lax.optimization_barrier(jnp.sum(r2 * r2, 0)) + CORE)
    step_sq = lax.optimization_barrier(jnp.sum(step * step, 0))
    along = lax.optimization_barrier(jnp.sum(step * (r1 / norm_one - r2 / norm_two), 0))
    weight = gamma * along / (FOUR_PI * (cross_sq + CORE * step_sq + CORE * CORE))
    return jnp.stack([lax.optimization_barrier(jnp.sum(weight * cross_x, 1)), lax.optimization_barrier(jnp.sum(weight * cross_y, 1)), lax.optimization_barrier(jnp.sum(weight * cross_z, 1))])

def spanned(points, segs, width):
    count = segs.shape[1]
    if count > width and count % width == 0:

        def add_part(index, total):
            part = lax.dynamic_slice_in_dim(segs, index * width, width, 1)
            return total + pair_velocity(points, part)
        return lax.fori_loop(0, count // width, add_part, jnp.zeros((3, points.shape[1]), jnp.float32))
    return pair_velocity(points, segs)

def sweep(padded, rhs, dgl):
    zpad = jnp.pad(padded, ((0, 0), (0, 0), (0, 0), (1, 1)))
    center = padded[:, 1:-1, 1:-1, :]
    beside = zpad[:, 2:, 1:-1, 1:-1] + zpad[:, :-2, 1:-1, 1:-1]
    beside = beside + zpad[:, 1:-1, 2:, 1:-1] + zpad[:, 1:-1, :-2, 1:-1]
    beside = beside + zpad[:, 1:-1, 1:-1, 2:] + zpad[:, 1:-1, 1:-1, :-2]
    resid = rhs - (dgl * center - beside)
    return center + OMEGA * resid / dgl

def reference(bnd_pos, bnd_owner, bnd_slot, seg_start, seg_step, seg_gamma, seg_sec, flow, source, extra_diag, circ_weight, sec_block, sec_row):
    wakes = [jnp.concatenate([seg_start[:, j], seg_step[:, j], seg_gamma[j][None]], 0) for j in range(BLADES)]
    blocks = jnp.moveaxis(bnd_pos.reshape(3, N_BLK, NB_DEV), 1, 0)

    def one_block(points):
        total = jnp.zeros((3, NB_DEV), jnp.float32)
        for j in range(BLADES):
            total = total + spanned(points, wakes[j], 2048)
        return total
    velocity = jnp.moveaxis(lax.map(one_block, blocks), 0, 1).reshape(3, NB)
    owner = bnd_owner[:, 0]
    row_y = bnd_slot // CZ
    row_z = bnd_slot % CZ
    face = jnp.zeros((3, N_BLK, NY, CZ), jnp.float32).at[:, owner, row_y, row_z].add(velocity)
    rhs = source.reshape(3, N_BLK, CX, NY, CZ).at[:, :, 0].add(face).reshape(3, NX, NY, CZ)
    dgl = 6.0 + extra_diag
    state = flow
    for step in range(PASSES):
        padded = jnp.pad(state, ((0, 0), (1, 1), (1, 1), (0, 0)))
        state = sweep(padded, rhs, dgl)
    profile = lax.optimization_barrier(jnp.sum((circ_weight * state[1]).reshape(N_BLK, CX, NY, CZ), axis=(1, 3)))
    rows = jnp.arange(BLADES, dtype=jnp.int32)[:, None] * CY + sec_row
    section = profile[sec_block, rows]
    looked = jnp.take_along_axis(section, seg_sec, axis=1)
    new_gamma = (1.0 - RELAX) * seg_gamma + RELAX * looked
    return (state, new_gamma)
```

```python
import functools
import math

import jax
import jax.numpy as jnp
from jax import lax
from jax.experimental import pallas as pl
from jax.experimental.pallas import tpu as pltpu
from jax.sharding import PartitionSpec as P

CORE = 0.01
FOUR_PI = 4.0 * math.pi
OMEGA = 0.8
RELAX = 0.5
LANES = 128
MESH = pl.DeviceIdType.MESH


def kernel(
    n_blk,
    n_bld,
    pos_ref,
    own_ref,
    slot_ref,
    start_ref,
    step_ref,
    gam_ref,
    sec_ref,
    sblk_ref,
    srow_ref,
    flow_ref,
    src_ref,
    diag_ref,
    circ_ref,
    out_ref,
    ng_ref,
    gath,
    vel,
    prof,
    flow_v,
    mid_v,
    out_v,
    src_v,
    diag_v,
    circ_v,
    m_v,
    ysend,
    yrecv,
    dgn_v,
    pos8,
    post,
    pb,
    keys,
    zt,
    lhs,
    sem_in,
    sem_out,
    wake_send,
    wake_recv,
    vel_send,
    vel_recv,
    prof_send,
    prof_recv,
    halo_send,
    halo_recv,
):
    n = n_blk * n_bld
    b = lax.axis_index("blk")
    j = lax.axis_index("blade")
    me = b * n_bld + j
    _, cx, cy, cz = src_v.shape
    half = pb.shape[1]
    n_pair = n // 2
    zbits = cz.bit_length() - 1

    def dev(d):
        return (lax.div(d, n_bld), lax.rem(d, n_bld))

    loads = [
        pltpu.make_async_copy(flow_ref, flow_v.at[:, pl.ds(1, cx)], sem_in.at[0]),
        pltpu.make_async_copy(diag_ref, diag_v, sem_in.at[1]),
        pltpu.make_async_copy(src_ref, src_v, sem_in.at[2]),
        pltpu.make_async_copy(circ_ref, circ_v, sem_in.at[3]),
    ]
    for copy in loads:
        copy.start()

    barrier = pltpu.get_barrier_semaphore()

    @pl.loop(1, n)
    def _(i):
        pl.semaphore_signal(
            barrier, inc=1, device_id=dev(lax.rem(me + i, n)), device_id_type=MESH
        )

    lane1 = lax.broadcasted_iota(jnp.int32, (8, LANES), 1)
    low1 = lane1 < half
    slot_row = jnp.broadcast_to(
        slot_ref[pl.ds(lax.div(j, 2), 1), :].astype(jnp.float32), (8, LANES)
    )
    own_row = jnp.broadcast_to(
        own_ref[pl.ds(lax.div(j, 2), 1), :].astype(jnp.float32), (8, LANES)
    )
    mine_low = lax.rem(j, 2) == 0
    own_row = pltpu.roll(own_row, half, 1)
    first = jnp.where(low1, slot_row, own_row)
    second = jnp.where(low1, own_row, slot_row)
    tag = jnp.where(mine_low, first, second)
    gath[me, 0:3, :] = start_ref[:, 0, :]
    gath[me, 3:6, :] = step_ref[:, 0, :]
    gath[me, 6:7, :] = gam_ref[...]
    gath[me, 7:8, :] = tag[0:1, :]

    pl.semaphore_wait(barrier, n - 1)

    def wake_copy(dst, slot):
        return pltpu.make_async_remote_copy(
            src_ref=gath.at[me],
            dst_ref=gath.at[me],
            send_sem=wake_send.at[slot],
            recv_sem=wake_recv.at[me],
            device_id=dev(dst),
            device_id_type=MESH,
        )

    @pl.loop(1, n)
    def _(i):
        wake_copy(lax.rem(me + i, n), i).start()

    has = (b < n_blk - 1, b > 0, j < n_bld - 1, j > 0)
    nxt_b, prv_b = (b + 1, j), (b - 1, j)
    nxt_j, prv_j = (b, j + 1), (b, j - 1)

    def halo_copies(stage):
        base = 4 * stage
        to_next = flow_ref.at[:, cx - 1] if stage == 0 else mid_v.at[:, cx]
        to_prev = flow_ref.at[:, 0] if stage == 0 else mid_v.at[:, 1]
        grid = flow_v if stage == 0 else mid_v
        pairs = [
            (to_next, grid.at[:, 0], nxt_b, 0),
            (to_prev, grid.at[:, cx + 1], prv_b, 1),
            (ysend.at[stage, 0], yrecv.at[stage, 0], nxt_j, 2),
            (ysend.at[stage, 1], yrecv.at[stage, 1], prv_j, 3),
        ]
        return [
            pltpu.make_async_remote_copy(
                src_ref=s,
                dst_ref=d,
                send_sem=halo_send.at[base + k],
                recv_sem=halo_recv.at[base + k],
                device_id=to,
                device_id_type=MESH,
            )
            for s, d, to, k in pairs
        ]

    def guarded(cond, action):
        @pl.when(cond)
        def _():
            action()

    diag_copy = pltpu.make_async_remote_copy(
        src_ref=diag_ref.at[0],
        dst_ref=dgn_v,
        send_sem=halo_send.at[8],
        recv_sem=halo_recv.at[8],
        device_id=prv_b,
        device_id_type=MESH,
    )
    halo0 = halo_copies(0)
    halo1 = halo_copies(1)
    guarded(has[0], halo0[0].start)
    guarded(has[1], halo0[1].start)

    arrives = (has[1], has[0], has[3], has[2])

    @pl.when(b == 0)
    def _():
        flow_v[:, 0] = jnp.zeros((3, cy, cz), jnp.float32)
        mid_v[:, 0] = jnp.zeros((3, cy, cz), jnp.float32)

    @pl.when(b == n_blk - 1)
    def _():
        flow_v[:, cx + 1] = jnp.zeros((3, cy, cz), jnp.float32)
        mid_v[:, cx + 1] = jnp.zeros((3, cy, cz), jnp.float32)
        dgn_v[...] = jnp.zeros((cy, cz), jnp.float32)

    @pl.when(j == 0)
    def _():
        yrecv[:, 0] = jnp.zeros(yrecv.shape[:1] + yrecv.shape[2:], jnp.float32)

    @pl.when(j == n_bld - 1)
    def _():
        yrecv[:, 1] = jnp.zeros(yrecv.shape[:1] + yrecv.shape[2:], jnp.float32)

    loads[0].wait()
    loads[1].wait()
    for c in range(3):
        ysend[0, 0, c] = flow_v[c, 1 : cx + 1, cy - 1, :]
        ysend[0, 1, c] = flow_v[c, 1 : cx + 1, 0, :]
    ysend[0, 0, 3] = diag_v[:, cy - 1, :]
    ysend[0, 1, 3] = diag_v[:, 0, :]
    guarded(has[2], halo0[2].start)
    guarded(has[3], halo0[3].start)
    guarded(has[1], diag_copy.start)

    pos8[...] = jnp.zeros(pos8.shape, jnp.float32)
    pos8[0:3, :] = pos_ref[...]
    post[...] = pos8[...].T
    mine = post[pl.ds(pl.multiple_of(j * half, half), half), :]
    for c in range(3):
        pb[c] = jnp.broadcast_to(mine[:, c : c + 1], (half, LANES))

    n_sec = sblk_ref.shape[1]
    place = sblk_ref[pl.ds(j, 1), :] * cy + srow_ref[pl.ds(j, 1), :]
    place = jnp.broadcast_to(place.astype(jnp.float32), (n_sec, n_sec))
    eye = lax.broadcasted_iota(jnp.int32, (n_sec, n_sec), 0) == lax.broadcasted_iota(
        jnp.int32, (n_sec, n_sec), 1
    )
    place = jnp.sum(jnp.where(eye, place, 0.0), axis=1, keepdims=True)
    match = lax.broadcasted_iota(jnp.int32, (n_sec, LANES), 0) == sec_ref[...]
    seg_place = jnp.sum(jnp.where(match, place, 0.0), axis=0, keepdims=True)

    row_id = lax.broadcasted_iota(jnp.int32, (cy, cz), 0)
    col_id = lax.broadcasted_iota(jnp.int32, (cy, cz), 1)

    def beside_plane(u, left, right):
        total = jnp.where(row_id == 0, left, pltpu.roll(u, 1, 0))
        total += jnp.where(row_id == cy - 1, right, pltpu.roll(u, cy - 1, 0))
        total += jnp.where(col_id == 0, 0.0, pltpu.roll(u, 1, 1))
        total += jnp.where(col_id == cz - 1, 0.0, pltpu.roll(u, cz - 1, 1))
        return total

    def relaxed(grid, stage, c, x, m):
        u = grid[c, x + 1]
        left = yrecv[stage, 0, c, pl.ds(x, 1), :]
        right = yrecv[stage, 1, c, pl.ds(x, 1), :]
        beside = beside_plane(u, left, right) + grid[c, x] + grid[c, x + 2]
        return (1.0 - OMEGA) * u + m * (src_v[c, x] + beside)

    loads[2].wait()
    for k in range(4):
        guarded(arrives[k], halo0[k].wait_recv)

    @pl.loop(0, cx)
    def _(x):
        m = OMEGA / (6.0 + diag_v[x])
        m_v[x] = m
        for c in range(3):
            mid_v[c, x + 1] = relaxed(flow_v, 0, c, x, m)

    for c in range(3):
        ysend[1, 0, c] = mid_v[c, 1 : cx + 1, cy - 1, :]
        ysend[1, 1, c] = mid_v[c, 1 : cx + 1, 0, :]
    ysend[1, 0, 3] = jnp.zeros((cx, cz), jnp.float32)
    ysend[1, 1, 3] = jnp.zeros((cx, cz), jnp.float32)
    for k in range(4):
        guarded(has[k], halo1[k].start)

    def induce(src, acc):
        rows = [jnp.broadcast_to(gath[src, r : r + 1, :], (8, LANES)) for r in range(7)]
        sx, sy, sz, dx, dy, dz, gam = rows
        dd = dx * dx + dy * dy + dz * dz
        bias = CORE * dd + CORE * CORE
        gam = gam * (1.0 / FOUR_PI)
        acc = list(acc)
        for g in range(half // 8):
            part = slice(8 * g, 8 * g + 8)
            rx, ry, rz = pb[0, part] - sx, pb[1, part] - sy, pb[2, part] - sz
            along_one = dx * rx + dy * ry + dz * rz
            along_two = along_one - dd
            sq_one = rx * rx + ry * ry + rz * rz + CORE
            sq_two = sq_one - along_one - along_two
            along = along_one * lax.rsqrt(sq_one) - along_two * lax.rsqrt(sq_two)
            kx = dy * rz - dz * ry
            ky = dz * rx - dx * rz
            kz = dx * ry - dy * rx
            w = gam * along / (kx * kx + ky * ky + kz * kz + bias)
            acc[3 * g] += w * kx
            acc[3 * g + 1] += w * ky
            acc[3 * g + 2] += w * kz
        return tuple(acc)

    zero = jnp.zeros((8, LANES), jnp.float32)
    acc = induce(me, (zero,) * (3 * (half // 8)))

    def wake_step(i, acc):
        src = lax.rem(me + n - i, n)
        pltpu.make_async_remote_copy(
            src_ref=gath.at[src],
            dst_ref=gath.at[src],
            send_sem=wake_send.at[i],
            recv_sem=wake_recv.at[src],
            device_id=dev(src),
            device_id_type=MESH,
        ).wait_recv()
        return induce(src, acc)

    acc = lax.fori_loop(1, n, wake_step, acc)
    ax, ay, az = (jnp.concatenate(acc[c::3], axis=0) for c in range(3))
    vel[me, 0:1, :] = jnp.sum(jnp.concatenate([ax, ay], axis=0).T, axis=0, keepdims=True)
    vel[me, 1:2, :] = jnp.sum(jnp.concatenate([az, az], axis=0).T, axis=0, keepdims=True)

    def vel_copy(dst, slot):
        return pltpu.make_async_remote_copy(
            src_ref=vel.at[me],
            dst_ref=vel.at[me],
            send_sem=vel_send.at[slot],
            recv_sem=vel_recv.at[me],
            device_id=dev(dst),
            device_id_type=MESH,
        )

    @pl.loop(1, n)
    def _(i):
        vel_copy(lax.rem(me + i, n), i).start()

    loads[3].wait()
    for k in range(4):
        guarded(arrives[k], halo1[k].wait_recv)

    def second(x, total):
        m = m_v[x]
        for c in range(3):
            u = relaxed(mid_v, 1, c, x, m)
            out_v[c, x] = u
            if c == 1:
                total += circ_v[x] * u
        return total

    profile = lax.fori_loop(0, cx, second, jnp.zeros((cy, cz), jnp.float32))
    store_inner = pltpu.make_async_copy(
        out_v.at[:, pl.ds(2, cx - 3)], out_ref.at[:, pl.ds(2, cx - 3)], sem_out.at[0]
    )
    store_inner.start()

    z_id = lax.broadcasted_iota(jnp.int32, (cz, LANES), 0)

    @pl.loop(0, n_pair)
    def _(q):
        even = jnp.broadcast_to(gath[2 * q, 7:8, :], (8, LANES))
        odd = jnp.broadcast_to(gath[2 * q + 1, 7:8, :], (8, LANES))
        slot = jnp.where(low1, even, odd).astype(jnp.int32)
        owner = pltpu.roll(jnp.where(low1, odd, even), half, 1).astype(jnp.int32)
        row = (slot >> zbits) - j * cy
        col = slot & (cz - 1)
        keys[q, 0] = jnp.where(owner == b, row, -4 * cy * n_bld)
        keys[q, 1] = jnp.where(owner == b + 1, row, -4 * cy * n_bld)
        cols = pl.ds(pl.multiple_of(q * LANES, LANES), LANES)
        zt[:, cols] = jnp.where(z_id == col[0:1, :], 1.0, 0.0).astype(jnp.bfloat16)

    y_id = lax.broadcasted_iota(jnp.int32, (cy, LANES), 0)
    edge_id = jnp.where(y_id >= 6, -2, jnp.where((y_id & 1) == 0, -1, cy))

    def vel_wait(i, carry):
        src = lax.rem(me + n - i, n)
        pltpu.make_async_remote_copy(
            src_ref=vel.at[src],
            dst_ref=vel.at[src],
            send_sem=vel_send.at[i],
            recv_sem=vel_recv.at[src],
            device_id=dev(src),
            device_id_type=MESH,
        ).wait_recv()
        return carry

    lax.fori_loop(1, n, vel_wait, 0)

    n_row = 7 * cy

    @pl.loop(0, n_pair)
    def _(q):
        e0 = jnp.broadcast_to(vel[2 * q, 0:1, :], (8, LANES))
        e1 = jnp.broadcast_to(vel[2 * q, 1:2, :], (8, LANES))
        o0 = jnp.broadcast_to(vel[2 * q + 1, 0:1, :], (8, LANES))
        o1 = jnp.broadcast_to(vel[2 * q + 1, 1:2, :], (8, LANES))
        v = (
            jnp.where(low1, e0, pltpu.roll(o0, half, 1))[0:1],
            jnp.where(low1, pltpu.roll(e0, half, 1), o0)[0:1],
            jnp.where(low1, e1, o1)[0:1],
        )
        key_own = keys[q, 0, 0:1, :]
        key_next = keys[q, 1, 0:1, :]
        own = y_id == key_own
        nxt = y_id == key_next
        edge = edge_id == key_own
        v_edge = jnp.where(y_id < 2, v[0], jnp.where(y_id < 4, v[1], v[2]))
        parts = [jnp.where(own, v[c], 0.0) for c in range(3)]
        parts += [jnp.where(nxt, v[c], 0.0) for c in range(3)]
        parts += [jnp.where(edge, v_edge, 0.0)]
        cols = pl.ds(pl.multiple_of(q * LANES, LANES), LANES)
        for k, part in enumerate(parts):
            high = part.astype(jnp.bfloat16)
            rest = (part - high.astype(jnp.float32)).astype(jnp.bfloat16)
            lhs[k * cy : (k + 1) * cy, cols] = high
            lhs[n_row + k * cy : n_row + (k + 1) * cy, cols] = rest

    dot = lax.dot_general(
        lhs[...], zt[...], (((1,), (1,)), ((), ())), preferred_element_type=jnp.float32
    )
    face = dot[:n_row] + dot[n_row:]

    guarded(has[0], diag_copy.wait_recv)
    m_first, m_second, m_last = m_v[0], m_v[1], m_v[cx - 1]
    m_next = OMEGA / (6.0 + dgn_v[...])
    m_left = OMEGA / (6.0 + yrecv[0, 0, 3, 0:1, :])
    m_right = OMEGA / (6.0 + yrecv[0, 1, 3, 0:1, :])
    for c in (1, 0, 2):
        one = m_first * face[c * cy : (c + 1) * cy]
        one_next = m_next * face[(3 + c) * cy : (4 + c) * cy]
        base = 6 * cy + 2 * c
        left = m_left * face[base : base + 1]
        right = m_right * face[base + 1 : base + 2]
        add_first = (2.0 - OMEGA) * one + m_first * beside_plane(one, left, right)
        add_second = m_second * one
        add_last = m_last * one_next
        if c == 1:
            profile += circ_v[0] * add_first + circ_v[1] * add_second
            profile += circ_v[cx - 1] * add_last
            prof[b] = jnp.broadcast_to(jnp.sum(profile, axis=1, keepdims=True), (cy, LANES))

            def prof_copy(dst, slot):
                return pltpu.make_async_remote_copy(
                    src_ref=prof.at[b],
                    dst_ref=prof.at[b],
                    send_sem=prof_send.at[slot],
                    recv_sem=prof_recv.at[b],
                    device_id=(dst, j),
                    device_id_type=MESH,
                )

            @pl.loop(1, n_blk)
            def _(i):
                prof_copy(lax.rem(b + i, n_blk), i).start()

        out_v[c, 0] += add_first
        out_v[c, 1] += add_second
        out_v[c, cx - 1] += add_last

    store_low = pltpu.make_async_copy(
        out_v.at[:, pl.ds(0, 2)], out_ref.at[:, pl.ds(0, 2)], sem_out.at[1]
    )
    store_high = pltpu.make_async_copy(
        out_v.at[:, pl.ds(cx - 1, 1)], out_ref.at[:, pl.ds(cx - 1, 1)], sem_out.at[2]
    )
    store_low.start()
    store_high.start()

    @pl.loop(1, n)
    def _(i):
        wake_copy(lax.rem(me + i, n), i).wait_send()
        vel_copy(lax.rem(me + i, n), i).wait_send()

    for k in range(4):
        guarded(has[k], halo0[k].wait_send)
        guarded(has[k], halo1[k].wait_send)
    guarded(has[1], diag_copy.wait_send)

    @pl.loop(1, n_blk)
    def _(i):
        src = lax.rem(b + n_blk - i, n_blk)
        pltpu.make_async_remote_copy(
            src_ref=prof.at[src],
            dst_ref=prof.at[src],
            send_sem=prof_send.at[i],
            recv_sem=prof_recv.at[src],
            device_id=(src, j),
            device_id_type=MESH,
        ).wait_recv()

    table = prof[...].reshape(n_blk * cy, LANES)
    spot = lax.broadcasted_iota(jnp.int32, (n_blk * cy, LANES), 0) == seg_place.astype(jnp.int32)
    looked = jnp.sum(jnp.where(spot, table, 0.0), axis=0, keepdims=True)
    ng_ref[...] = (1.0 - RELAX) * gam_ref[...] + RELAX * looked

    @pl.loop(1, n_blk)
    def _(i):
        prof_copy(lax.rem(b + i, n_blk), i).wait_send()

    store_inner.wait()
    store_low.wait()
    store_high.wait()


def per_device(
    n_blk,
    n_bld,
    bnd_pos,
    bnd_owner,
    bnd_slot,
    seg_start,
    seg_step,
    seg_gamma,
    seg_sec,
    flow,
    source,
    extra_diag,
    circ_weight,
    sec_block,
    sec_row,
):
    n = n_blk * n_bld
    _, cx, cy, cz = flow.shape
    cells = bnd_pos.shape[1]
    half = cells // n_bld
    n_cells = n * half
    f32 = jnp.float32
    vmem = pl.BlockSpec(memory_space=pltpu.VMEM)
    hbm = pl.BlockSpec(memory_space=pl.ANY)
    dma = pltpu.SemaphoreType.DMA
    return pl.pallas_call(
        functools.partial(kernel, n_blk, n_bld),
        out_shape=(
            jax.ShapeDtypeStruct(flow.shape, f32),
            jax.ShapeDtypeStruct(seg_gamma.shape, f32),
        ),
        in_specs=[vmem] * 9 + [hbm] * 4,
        out_specs=(hbm, vmem),
        scratch_shapes=[
            pltpu.VMEM((n, 8, LANES), f32),
            pltpu.VMEM((n, 2, LANES), f32),
            pltpu.VMEM((n_blk, cy, LANES), f32),
            pltpu.VMEM((3, cx + 2, cy, cz), f32),
            pltpu.VMEM((3, cx + 2, cy, cz), f32),
            pltpu.VMEM((3, cx, cy, cz), f32),
            pltpu.VMEM((3, cx, cy, cz), f32),
            pltpu.VMEM((cx, cy, cz), f32),
            pltpu.VMEM((cx, cy, cz), f32),
            pltpu.VMEM((cx, cy, cz), f32),
            pltpu.VMEM((2, 2, 4, cx, cz), f32),
            pltpu.VMEM((2, 2, 4, cx, cz), f32),
            pltpu.VMEM((cy, cz), f32),
            pltpu.VMEM((8, cells), f32),
            pltpu.VMEM((cells, 8), f32),
            pltpu.VMEM((3, half, LANES), f32),
            pltpu.VMEM((n // 2, 2, 8, LANES), jnp.int32),
            pltpu.VMEM((cz, n_cells), jnp.bfloat16),
            pltpu.VMEM((14 * cy, n_cells), jnp.bfloat16),
            dma((4,)),
            dma((3,)),
            dma((n,)),
            dma((n,)),
            dma((n,)),
            dma((n,)),
            dma((n_blk,)),
            dma((n_blk,)),
            dma((9,)),
            dma((9,)),
        ],
        compiler_params=pltpu.CompilerParams(
            collective_id=0, has_side_effects=True, vmem_limit_bytes=40 * 1024 * 1024
        ),
    )(
        bnd_pos,
        bnd_owner.reshape(cells // LANES, LANES),
        bnd_slot.reshape(cells // LANES, LANES),
        seg_start,
        seg_step,
        seg_gamma,
        seg_sec,
        sec_block,
        sec_row,
        flow,
        source,
        extra_diag,
        circ_weight,
    )


def solution(mesh):
    return jax.shard_map(
        functools.partial(per_device, mesh.shape["blk"], mesh.shape["blade"]),
        mesh=mesh,
        in_specs=(
            P(None, "blk"),
            P("blk", None),
            P("blk"),
            P(None, "blade", "blk"),
            P(None, "blade", "blk"),
            P("blade", "blk"),
            P("blade", "blk"),
            P(None, "blk", "blade", None),
            P(None, "blk", "blade", None),
            P("blk", "blade", None),
            P("blk", "blade", None),
            P(),
            P(),
        ),
        out_specs=(P(None, "blk", "blade", None), P("blade", "blk")),
        check_vma=False,
    )
```

```python
import functools
import math

import jax
import jax.numpy as jnp
from jax import lax
from jax.experimental import pallas as pl
from jax.experimental.pallas import tpu as pltpu
from jax.sharding import PartitionSpec as P

CORE = 0.01
FOUR_PI = 4.0 * math.pi
OMEGA = 0.8
RELAX = 0.5
LANES = 128
MESH = pl.DeviceIdType.MESH


def kernel(
    n_blk,
    n_bld,
    pos_hbm,
    own_hbm,
    slot_hbm,
    start_hbm,
    step_hbm,
    gam_hbm,
    sec_hbm,
    sblk_hbm,
    srow_hbm,
    flow_ref,
    src_ref,
    diag_ref,
    circ_ref,
    out_ref,
    ng_hbm,
    pos_ref,
    own_ref,
    slot_ref,
    start_ref,
    step_ref,
    gam_ref,
    sec_ref,
    sblk_ref,
    srow_ref,
    ng_ref,
    gath,
    vel,
    prof,
    flow_v,
    mid_v,
    out_v,
    src_v,
    diag_v,
    circ_v,
    m_v,
    ysend,
    yrecv,
    dgn_v,
    pos8,
    post,
    pb,
    keys,
    zt,
    lhs,
    sem_in,
    sem_out,
    wake_send,
    wake_recv,
    vel_send,
    vel_recv,
    prof_send,
    prof_recv,
    halo_send,
    halo_recv,
):
    n = n_blk * n_bld
    b = lax.axis_index("blk")
    j = lax.axis_index("blade")
    me = b * n_bld + j
    _, cx, cy, cz = src_v.shape
    half = pb.shape[1]
    n_pair = n // 2
    zbits = cz.bit_length() - 1

    def dev(d):
        return (lax.div(d, n_bld), lax.rem(d, n_bld))

    small = [
        pltpu.make_async_copy(source, target, sem_in.at[4 + k])
        for k, (source, target) in enumerate(
            (
                (start_hbm, start_ref),
                (step_hbm, step_ref),
                (gam_hbm, gam_ref),
                (slot_hbm, slot_ref),
                (own_hbm, own_ref),
                (pos_hbm, pos_ref),
                (sec_hbm, sec_ref),
                (sblk_hbm, sblk_ref),
                (srow_hbm, srow_ref),
            )
        )
    ]
    for copy in small:
        copy.start()
    loads = [
        pltpu.make_async_copy(flow_ref, flow_v.at[:, pl.ds(1, cx)], sem_in.at[0]),
        pltpu.make_async_copy(diag_ref, diag_v, sem_in.at[1]),
        pltpu.make_async_copy(src_ref, src_v, sem_in.at[2]),
        pltpu.make_async_copy(circ_ref, circ_v, sem_in.at[3]),
    ]
    for copy in loads:
        copy.start()

    barrier = pltpu.get_barrier_semaphore()

    @pl.loop(1, n)
    def _(i):
        pl.semaphore_signal(
            barrier, inc=1, device_id=dev(lax.rem(me + i, n)), device_id_type=MESH
        )

    for copy in small:
        copy.wait()

    lane1 = lax.broadcasted_iota(jnp.int32, (8, LANES), 1)
    low1 = lane1 < half
    slot_row = jnp.broadcast_to(
        slot_ref[pl.ds(lax.div(j, 2), 1), :].astype(jnp.float32), (8, LANES)
    )
    own_row = jnp.broadcast_to(
        own_ref[pl.ds(lax.div(j, 2), 1), :].astype(jnp.float32), (8, LANES)
    )
    mine_low = lax.rem(j, 2) == 0
    own_row = pltpu.roll(own_row, half, 1)
    first = jnp.where(low1, slot_row, own_row)
    second = jnp.where(low1, own_row, slot_row)
    tag = jnp.where(mine_low, first, second)
    gath[me, 0:3, :] = start_ref[:, 0, :]
    gath[me, 3:6, :] = step_ref[:, 0, :]
    gath[me, 6:7, :] = gam_ref[...]
    gath[me, 7:8, :] = tag[0:1, :]

    pl.semaphore_wait(barrier, n - 1)

    def wake_copy(dst, slot):
        return pltpu.make_async_remote_copy(
            src_ref=gath.at[me],
            dst_ref=gath.at[me],
            send_sem=wake_send.at[slot],
            recv_sem=wake_recv.at[me],
            device_id=dev(dst),
            device_id_type=MESH,
        )

    @pl.loop(1, n)
    def _(i):
        wake_copy(lax.rem(me + i, n), i).start()

    has = (b < n_blk - 1, b > 0, j < n_bld - 1, j > 0)
    nxt_b, prv_b = (b + 1, j), (b - 1, j)
    nxt_j, prv_j = (b, j + 1), (b, j - 1)

    def halo_copies(stage):
        base = 4 * stage
        to_next = flow_ref.at[:, cx - 1] if stage == 0 else mid_v.at[:, cx]
        to_prev = flow_ref.at[:, 0] if stage == 0 else mid_v.at[:, 1]
        grid = flow_v if stage == 0 else mid_v
        pairs = [
            (to_next, grid.at[:, 0], nxt_b, 0),
            (to_prev, grid.at[:, cx + 1], prv_b, 1),
            (ysend.at[stage, 0], yrecv.at[stage, 0], nxt_j, 2),
            (ysend.at[stage, 1], yrecv.at[stage, 1], prv_j, 3),
        ]
        return [
            pltpu.make_async_remote_copy(
                src_ref=s,
                dst_ref=d,
                send_sem=halo_send.at[base + k],
                recv_sem=halo_recv.at[base + k],
                device_id=to,
                device_id_type=MESH,
            )
            for s, d, to, k in pairs
        ]

    def guarded(cond, action):
        @pl.when(cond)
        def _():
            action()

    diag_copy = pltpu.make_async_remote_copy(
        src_ref=diag_ref.at[0],
        dst_ref=dgn_v,
        send_sem=halo_send.at[8],
        recv_sem=halo_recv.at[8],
        device_id=prv_b,
        device_id_type=MESH,
    )
    halo0 = halo_copies(0)
    halo1 = halo_copies(1)
    guarded(has[0], halo0[0].start)
    guarded(has[1], halo0[1].start)

    arrives = (has[1], has[0], has[3], has[2])

    @pl.when(b == 0)
    def _():
        flow_v[:, 0] = jnp.zeros((3, cy, cz), jnp.float32)
        mid_v[:, 0] = jnp.zeros((3, cy, cz), jnp.float32)

    @pl.when(b == n_blk - 1)
    def _():
        flow_v[:, cx + 1] = jnp.zeros((3, cy, cz), jnp.float32)
        mid_v[:, cx + 1] = jnp.zeros((3, cy, cz), jnp.float32)
        dgn_v[...] = jnp.zeros((cy, cz), jnp.float32)

    @pl.when(j == 0)
    def _():
        yrecv[:, 0] = jnp.zeros(yrecv.shape[:1] + yrecv.shape[2:], jnp.float32)

    @pl.when(j == n_bld - 1)
    def _():
        yrecv[:, 1] = jnp.zeros(yrecv.shape[:1] + yrecv.shape[2:], jnp.float32)

    loads[0].wait()
    loads[1].wait()
    for c in range(3):
        ysend[0, 0, c] = flow_v[c, 1 : cx + 1, cy - 1, :]
        ysend[0, 1, c] = flow_v[c, 1 : cx + 1, 0, :]
    ysend[0, 0, 3] = diag_v[:, cy - 1, :]
    ysend[0, 1, 3] = diag_v[:, 0, :]
    guarded(has[2], halo0[2].start)
    guarded(has[3], halo0[3].start)
    guarded(has[1], diag_copy.start)

    pos8[...] = jnp.zeros(pos8.shape, jnp.float32)
    pos8[0:3, :] = pos_ref[...]
    post[...] = pos8[...].T
    mine = post[pl.ds(pl.multiple_of(j * half, half), half), :]
    for c in range(3):
        pb[c] = jnp.broadcast_to(mine[:, c : c + 1], (half, LANES))

    n_sec = sblk_ref.shape[1]
    place = sblk_ref[pl.ds(j, 1), :] * cy + srow_ref[pl.ds(j, 1), :]
    place = jnp.broadcast_to(place.astype(jnp.float32), (n_sec, n_sec))
    eye = lax.broadcasted_iota(jnp.int32, (n_sec, n_sec), 0) == lax.broadcasted_iota(
        jnp.int32, (n_sec, n_sec), 1
    )
    place = jnp.sum(jnp.where(eye, place, 0.0), axis=1, keepdims=True)
    match = lax.broadcasted_iota(jnp.int32, (n_sec, LANES), 0) == sec_ref[...]
    seg_place = jnp.sum(jnp.where(match, place, 0.0), axis=0, keepdims=True)

    row_id = lax.broadcasted_iota(jnp.int32, (cy, cz), 0)
    col_id = lax.broadcasted_iota(jnp.int32, (cy, cz), 1)

    def beside_plane(u, left, right):
        total = jnp.where(row_id == 0, left, pltpu.roll(u, 1, 0))
        total += jnp.where(row_id == cy - 1, right, pltpu.roll(u, cy - 1, 0))
        total += jnp.where(col_id == 0, 0.0, pltpu.roll(u, 1, 1))
        total += jnp.where(col_id == cz - 1, 0.0, pltpu.roll(u, cz - 1, 1))
        return total

    def relaxed(grid, stage, c, x, m):
        u = grid[c, x + 1]
        left = yrecv[stage, 0, c, pl.ds(x, 1), :]
        right = yrecv[stage, 1, c, pl.ds(x, 1), :]
        beside = beside_plane(u, left, right) + grid[c, x] + grid[c, x + 2]
        return (1.0 - OMEGA) * u + m * (src_v[c, x] + beside)

    def induce(src, acc):
        rows = [jnp.broadcast_to(gath[src, r : r + 1, :], (8, LANES)) for r in range(7)]
        sx, sy, sz, dx, dy, dz, gam = rows
        dd = dx * dx + dy * dy + dz * dz
        bias = CORE * dd + CORE * CORE
        gam = gam * (1.0 / FOUR_PI)
        acc = list(acc)
        for g in range(half // 8):
            part = slice(8 * g, 8 * g + 8)
            rx, ry, rz = pb[0, part] - sx, pb[1, part] - sy, pb[2, part] - sz
            along_one = dx * rx + dy * ry + dz * rz
            along_two = along_one - dd
            sq_one = rx * rx + ry * ry + rz * rz + CORE
            sq_two = sq_one - along_one - along_two
            along = along_one * lax.rsqrt(sq_one) - along_two * lax.rsqrt(sq_two)
            kx = dy * rz - dz * ry
            ky = dz * rx - dx * rz
            kz = dx * ry - dy * rx
            w = gam * along / (kx * kx + ky * ky + kz * kz + bias)
            acc[3 * g] += w * kx
            acc[3 * g + 1] += w * ky
            acc[3 * g + 2] += w * kz
        return tuple(acc)

    zero = jnp.zeros((8, LANES), jnp.float32)
    acc = induce(me, (zero,) * (3 * (half // 8)))

    def wake_step(i, acc):
        src = lax.rem(me + n - i, n)
        pltpu.make_async_remote_copy(
            src_ref=gath.at[src],
            dst_ref=gath.at[src],
            send_sem=wake_send.at[i],
            recv_sem=wake_recv.at[src],
            device_id=dev(src),
            device_id_type=MESH,
        ).wait_recv()
        return induce(src, acc)

    middle = n // 2
    acc = lax.fori_loop(1, middle, wake_step, acc)

    loads[2].wait()
    for k in range(4):
        guarded(arrives[k], halo0[k].wait_recv)

    @pl.loop(0, cx)
    def _(x):
        m = OMEGA / (6.0 + diag_v[x])
        m_v[x] = m
        for c in range(3):
            mid_v[c, x + 1] = relaxed(flow_v, 0, c, x, m)

    for c in range(3):
        ysend[1, 0, c] = mid_v[c, 1 : cx + 1, cy - 1, :]
        ysend[1, 1, c] = mid_v[c, 1 : cx + 1, 0, :]
    ysend[1, 0, 3] = jnp.zeros((cx, cz), jnp.float32)
    ysend[1, 1, 3] = jnp.zeros((cx, cz), jnp.float32)
    for k in range(4):
        guarded(has[k], halo1[k].start)

    acc = lax.fori_loop(middle, n, wake_step, acc)
    ax, ay, az = (jnp.concatenate(acc[c::3], axis=0) for c in range(3))
    vel[me, 0:1, :] = jnp.sum(jnp.concatenate([ax, ay], axis=0).T, axis=0, keepdims=True)
    vel[me, 1:2, :] = jnp.sum(jnp.concatenate([az, az], axis=0).T, axis=0, keepdims=True)

    def vel_copy(dst, slot):
        return pltpu.make_async_remote_copy(
            src_ref=vel.at[me],
            dst_ref=vel.at[me],
            send_sem=vel_send.at[slot],
            recv_sem=vel_recv.at[me],
            device_id=dev(dst),
            device_id_type=MESH,
        )

    @pl.loop(1, n)
    def _(i):
        vel_copy(lax.rem(me + i, n), i).start()

    loads[3].wait()
    for k in range(4):
        guarded(arrives[k], halo1[k].wait_recv)

    def second(x, total):
        m = m_v[x]
        for c in range(3):
            u = relaxed(mid_v, 1, c, x, m)
            out_v[c, x] = u
            if c == 1:
                total += circ_v[x] * u
        return total

    profile = lax.fori_loop(0, cx, second, jnp.zeros((cy, cz), jnp.float32))
    store_inner = pltpu.make_async_copy(
        out_v.at[:, pl.ds(2, cx - 3)], out_ref.at[:, pl.ds(2, cx - 3)], sem_out.at[0]
    )
    store_inner.start()

    z_id = lax.broadcasted_iota(jnp.int32, (cz, LANES), 0)

    @pl.loop(0, n_pair, unroll=4)
    def _(q):
        even = jnp.broadcast_to(gath[2 * q, 7:8, :], (8, LANES))
        odd = jnp.broadcast_to(gath[2 * q + 1, 7:8, :], (8, LANES))
        slot = jnp.where(low1, even, odd).astype(jnp.int32)
        owner = pltpu.roll(jnp.where(low1, odd, even), half, 1).astype(jnp.int32)
        row = (slot >> zbits) - j * cy
        col = slot & (cz - 1)
        keys[q, 0] = jnp.where(owner == b, row, -4 * cy * n_bld)
        keys[q, 1] = jnp.where(owner == b + 1, row, -4 * cy * n_bld)
        cols = pl.ds(pl.multiple_of(q * LANES, LANES), LANES)
        zt[:, cols] = jnp.where(z_id == col[0:1, :], 1.0, 0.0).astype(jnp.bfloat16)

    y_id = lax.broadcasted_iota(jnp.int32, (cy, LANES), 0)
    edge_id = jnp.where(y_id >= 6, -2, jnp.where((y_id & 1) == 0, -1, cy))

    def vel_wait(i, carry):
        src = lax.rem(me + n - i, n)
        pltpu.make_async_remote_copy(
            src_ref=vel.at[src],
            dst_ref=vel.at[src],
            send_sem=vel_send.at[i],
            recv_sem=vel_recv.at[src],
            device_id=dev(src),
            device_id_type=MESH,
        ).wait_recv()
        return carry

    lax.fori_loop(1, n, vel_wait, 0)

    n_row = 7 * cy

    @pl.loop(0, n_pair, unroll=4)
    def _(q):
        e0 = jnp.broadcast_to(vel[2 * q, 0:1, :], (8, LANES))
        e1 = jnp.broadcast_to(vel[2 * q, 1:2, :], (8, LANES))
        o0 = jnp.broadcast_to(vel[2 * q + 1, 0:1, :], (8, LANES))
        o1 = jnp.broadcast_to(vel[2 * q + 1, 1:2, :], (8, LANES))
        v = (
            jnp.where(low1, e0, pltpu.roll(o0, half, 1))[0:1],
            jnp.where(low1, pltpu.roll(e0, half, 1), o0)[0:1],
            jnp.where(low1, e1, o1)[0:1],
        )
        key_own = keys[q, 0, 0:1, :]
        key_next = keys[q, 1, 0:1, :]
        own = y_id == key_own
        nxt = y_id == key_next
        edge = edge_id == key_own
        v_edge = jnp.where(y_id < 2, v[0], jnp.where(y_id < 4, v[1], v[2]))
        parts = [jnp.where(own, v[c], 0.0) for c in range(3)]
        parts += [jnp.where(nxt, v[c], 0.0) for c in range(3)]
        parts += [jnp.where(edge, v_edge, 0.0)]
        cols = pl.ds(pl.multiple_of(q * LANES, LANES), LANES)
        for k, part in enumerate(parts):
            high = part.astype(jnp.bfloat16)
            rest = (part - high.astype(jnp.float32)).astype(jnp.bfloat16)
            lhs[k * cy : (k + 1) * cy, cols] = high
            lhs[n_row + k * cy : n_row + (k + 1) * cy, cols] = rest

    dot = lax.dot_general(
        lhs[...], zt[...], (((1,), (1,)), ((), ())), preferred_element_type=jnp.float32
    )
    face = dot[:n_row] + dot[n_row:]

    guarded(has[0], diag_copy.wait_recv)
    m_first, m_second, m_last = m_v[0], m_v[1], m_v[cx - 1]
    m_next = OMEGA / (6.0 + dgn_v[...])
    m_left = OMEGA / (6.0 + yrecv[0, 0, 3, 0:1, :])
    m_right = OMEGA / (6.0 + yrecv[0, 1, 3, 0:1, :])
    for c in (1, 0, 2):
        one = m_first * face[c * cy : (c + 1) * cy]
        one_next = m_next * face[(3 + c) * cy : (4 + c) * cy]
        base = 6 * cy + 2 * c
        left = m_left * face[base : base + 1]
        right = m_right * face[base + 1 : base + 2]
        add_first = (2.0 - OMEGA) * one + m_first * beside_plane(one, left, right)
        add_second = m_second * one
        add_last = m_last * one_next
        if c == 1:
            profile += circ_v[0] * add_first + circ_v[1] * add_second
            profile += circ_v[cx - 1] * add_last
            folded = sum(profile[:, k : k + LANES] for k in range(0, cz, LANES))
            folded = jnp.concatenate([folded, jnp.zeros((LANES - cy, LANES), jnp.float32)], axis=0)
            prof[b] = jnp.sum(folded.T, axis=0, keepdims=True)

            def prof_copy(dst, slot):
                return pltpu.make_async_remote_copy(
                    src_ref=prof.at[b],
                    dst_ref=prof.at[b],
                    send_sem=prof_send.at[slot],
                    recv_sem=prof_recv.at[b],
                    device_id=(dst, j),
                    device_id_type=MESH,
                )

            @pl.loop(1, n_blk)
            def _(i):
                prof_copy(lax.rem(b + i, n_blk), i).start()

        out_v[c, 0] += add_first
        out_v[c, 1] += add_second
        out_v[c, cx - 1] += add_last

    store_low = pltpu.make_async_copy(
        out_v.at[:, pl.ds(0, 2)], out_ref.at[:, pl.ds(0, 2)], sem_out.at[1]
    )
    store_high = pltpu.make_async_copy(
        out_v.at[:, pl.ds(cx - 1, 1)], out_ref.at[:, pl.ds(cx - 1, 1)], sem_out.at[2]
    )
    store_low.start()
    store_high.start()

    @pl.loop(1, n)
    def _(i):
        wake_copy(lax.rem(me + i, n), i).wait_send()
        vel_copy(lax.rem(me + i, n), i).wait_send()

    for k in range(4):
        guarded(has[k], halo0[k].wait_send)
        guarded(has[k], halo1[k].wait_send)
    guarded(has[1], diag_copy.wait_send)

    @pl.loop(1, n_blk)
    def _(i):
        src = lax.rem(b + n_blk - i, n_blk)
        pltpu.make_async_remote_copy(
            src_ref=prof.at[src],
            dst_ref=prof.at[src],
            send_sem=prof_send.at[i],
            recv_sem=prof_recv.at[src],
            device_id=(src, j),
            device_id_type=MESH,
        ).wait_recv()

    table = prof[:, 0, :].T
    place_id = seg_place.astype(jnp.int32)
    looked = jnp.zeros((cy, LANES), jnp.float32)
    for k in range(n_blk):
        looked += jnp.where(y_id + k * cy == place_id, table[:cy, k : k + 1], 0.0)
    looked = jnp.sum(looked, axis=0, keepdims=True)
    ng_ref[...] = (1.0 - RELAX) * gam_ref[...] + RELAX * looked
    store_ng = pltpu.make_async_copy(ng_ref, ng_hbm, sem_out.at[3])
    store_ng.start()

    @pl.loop(1, n_blk)
    def _(i):
        prof_copy(lax.rem(b + i, n_blk), i).wait_send()

    store_inner.wait()
    store_low.wait()
    store_high.wait()
    store_ng.wait()


def per_device(
    n_blk,
    n_bld,
    bnd_pos,
    bnd_owner,
    bnd_slot,
    seg_start,
    seg_step,
    seg_gamma,
    seg_sec,
    flow,
    source,
    extra_diag,
    circ_weight,
    sec_block,
    sec_row,
):
    n = n_blk * n_bld
    _, cx, cy, cz = flow.shape
    cells = bnd_pos.shape[1]
    half = cells // n_bld
    n_cells = n * half
    f32 = jnp.float32
    hbm = pl.BlockSpec(memory_space=pltpu.HBM)
    dma = pltpu.SemaphoreType.DMA
    return pl.pallas_call(
        functools.partial(kernel, n_blk, n_bld),
        out_shape=(
            jax.ShapeDtypeStruct(flow.shape, f32),
            jax.ShapeDtypeStruct(seg_gamma.shape, f32),
        ),
        in_specs=[hbm] * 13,
        out_specs=(hbm, hbm),
        scratch_shapes=[
            pltpu.VMEM(bnd_pos.shape, f32),
            pltpu.VMEM((cells // LANES, LANES), jnp.int32),
            pltpu.VMEM((cells // LANES, LANES), jnp.int32),
            pltpu.VMEM(seg_start.shape, f32),
            pltpu.VMEM(seg_step.shape, f32),
            pltpu.VMEM(seg_gamma.shape, f32),
            pltpu.VMEM(seg_sec.shape, jnp.int32),
            pltpu.VMEM(sec_block.shape, jnp.int32),
            pltpu.VMEM(sec_row.shape, jnp.int32),
            pltpu.VMEM(seg_gamma.shape, f32),
            pltpu.VMEM((n, 8, LANES), f32),
            pltpu.VMEM((n, 2, LANES), f32),
            pltpu.VMEM((n_blk, 1, LANES), f32),
            pltpu.VMEM((3, cx + 2, cy, cz), f32),
            pltpu.VMEM((3, cx + 2, cy, cz), f32),
            pltpu.VMEM((3, cx, cy, cz), f32),
            pltpu.VMEM((3, cx, cy, cz), f32),
            pltpu.VMEM((cx, cy, cz), f32),
            pltpu.VMEM((cx, cy, cz), f32),
            pltpu.VMEM((cx, cy, cz), f32),
            pltpu.VMEM((2, 2, 4, cx, cz), f32),
            pltpu.VMEM((2, 2, 4, cx, cz), f32),
            pltpu.VMEM((cy, cz), f32),
            pltpu.VMEM((8, cells), f32),
            pltpu.VMEM((cells, 8), f32),
            pltpu.VMEM((3, half, LANES), f32),
            pltpu.VMEM((n // 2, 2, 8, LANES), jnp.int32),
            pltpu.VMEM((cz, n_cells), jnp.bfloat16),
            pltpu.VMEM((14 * cy, n_cells), jnp.bfloat16),
            dma((13,)),
            dma((4,)),
            dma((n,)),
            dma((n,)),
            dma((n,)),
            dma((n,)),
            dma((n_blk,)),
            dma((n_blk,)),
            dma((9,)),
            dma((9,)),
        ],
        compiler_params=pltpu.CompilerParams(
            collective_id=0, has_side_effects=True, vmem_limit_bytes=56 * 1024 * 1024
        ),
    )(
        bnd_pos,
        bnd_owner.reshape(cells // LANES, LANES),
        bnd_slot.reshape(cells // LANES, LANES),
        seg_start,
        seg_step,
        seg_gamma,
        seg_sec,
        sec_block,
        sec_row,
        flow,
        source,
        extra_diag,
        circ_weight,
    )


def solution(mesh):
    return jax.shard_map(
        functools.partial(per_device, mesh.shape["blk"], mesh.shape["blade"]),
        mesh=mesh,
        in_specs=(
            P(None, "blk"),
            P("blk", None),
            P("blk"),
            P(None, "blade", "blk"),
            P(None, "blade", "blk"),
            P("blade", "blk"),
            P("blade", "blk"),
            P(None, "blk", "blade", None),
            P(None, "blk", "blade", None),
            P("blk", "blade", None),
            P("blk", "blade", None),
            P(),
            P(),
        ),
        out_specs=(P(None, "blk", "blade", None), P("blade", "blk")),
        check_vma=False,
    )
```
